32 devices in a mesh: ctx: 16 (over z, y, core), tp: 2 (over x).
Axes of the slice: x: 2, y: 2, z: 4, core: 2. Of those that a mesh axis runs over, the one named last changes fastest.
Arguments:
- queries: bfloat16 [2048, 2048], P('ctx', 'tp'), may hold values from -200 to 200, as said below
- key_rows: bfloat16 [2048, 256], P('ctx', 'tp'), may hold values from -6 to 6
- value_rows: bfloat16 [2048, 256], P('ctx', 'tp'), may hold values from -6 to 6
- retained: int32 [16, 2, 16], P('ctx', 'tp'), may hold values from 0 to 127, as said below
Outputs:
- context: bfloat16 [2048, 2048], P(('ctx', 'tp'))
The draws below stay inside these ranges and needn't reach their ends.
Inputs may be any that keep to these rules, and one draw needn't show every extreme that they name: `queries`: queries of order one; some rows may be large multiples of earlier keys. `retained`: each list holds 16 different row numbers of its block in increasing order, always the first row 0 and the last row 127.
All inputs are finite; a program needn't handle non-finite values.
Results may differ from the reference program's by a relative error of at most 0.0033.
Values may be sent and summed in bfloat16 or wider, within the bound.
A program may use at most 64 MiB of HBM per device.

```python
import math
import jax
import jax.numpy as jnp
from jax import lax

HD = 128
GROUP = 8
BLOCK = 128
KVH = 2
KEEP = 16
TOKENS = 2048


def shared_keys(key):
    base = jax.random.normal(jax.random.fold_in(key, 11), (TOKENS, KVH, HD), jnp.float32)
    return jnp.clip(base, -5.9, 5.9)


def draw_key_rows(key, part):
    common = shared_keys(key)
    return common.reshape(TOKENS, KVH * HD).astype(jnp.bfloat16)


def draw_queries(key, part):
    key = jax.random.fold_in(key, 5)
    result = 2.5 * jax.random.normal(key, (TOKENS, KVH, GROUP, HD), jnp.float32)
    return result.reshape(TOKENS, KVH * GROUP * HD).astype(jnp.bfloat16)


def draw_retained(key, part):
    key = jax.random.fold_in(key, 9)
    list_count = TOKENS // BLOCK * KVH
    list_keys = jax.random.split(key, list_count)

    def one_list(list_key):
        middle_rows = jax.random.permutation(list_key, BLOCK - 2)[:KEEP - 2].astype(jnp.int32) + 1
        return jnp.concatenate([jnp.zeros((1,), jnp.int32), jnp.sort(middle_rows), jnp.full((1,), BLOCK - 1, jnp.int32)])
    return jax.vmap(one_list)(list_keys).reshape(TOKENS // BLOCK, KVH, KEEP)


def block_levels(own_key, extent, cuts, low, high):
    loudness, own = 1.0, jax.random.fold_in(own_key, 6)
    for dim, parts in cuts:
        heights = jnp.exp(jax.random.uniform(jax.random.fold_in(own, dim), (parts,), jnp.float32, low / len(cuts), high / len(cuts)))
        loudness = loudness * jnp.repeat(heights, extent[dim] // parts).reshape([-1 if axis == dim else 1 for axis in range(len(extent))])
    return loudness


def normal_values(rng, shape, width, limit, cuts=(), held_as=jnp.bfloat16):
    values = width * jax.random.normal(rng, shape, jnp.float32)
    if cuts:
        values = values * block_levels(rng, shape, cuts, -0.22, 0.18)
    return jnp.clip(values, -limit, limit).astype(held_as)


def setup_inputs(seed: int = 0) -> dict:
    splits = jax.random.split(jax.random.key(seed), 5)
    return {
        "queries": draw_queries(jax.random.fold_in(splits[4], 71), 0),
        "key_rows": draw_key_rows(jax.random.fold_in(splits[4], 71), 0),
        "value_rows": normal_values(splits[2], (TOKENS, KVH * HD), 1.0, 6.0, ((0, 16), (1, 2))),
        "retained": draw_retained(jax.random.fold_in(splits[4], 71), 0),
    }


def reference(queries, key_rows, value_rows, retained):
    hosts = TOKENS // BLOCK
    scale_factor = 1.0 / math.sqrt(HD)
    query_blocks = queries.reshape(hosts, BLOCK, KVH, GROUP, HD)
    key_blocks = key_rows.reshape(hosts, BLOCK, KVH, HD).transpose(0, 2, 1, 3)
    value_blocks = value_rows.reshape(hosts, BLOCK, KVH, HD).transpose(0, 2, 1, 3)
    picks = jnp.broadcast_to(retained[..., None], (hosts, KVH, KEEP, HD))
    kept_keys = jnp.take_along_axis(key_blocks, picks, axis=2)
    kept_values = jnp.take_along_axis(value_blocks, picks, axis=2)
    passing_keys = kept_keys.transpose(1, 0, 2, 3).reshape(KVH, hosts * KEEP, HD)
    passing_values = kept_values.transpose(1, 0, 2, 3).reshape(KVH, hosts * KEEP, HD)
    owners = jnp.arange(hosts * KEEP, dtype=jnp.int32) // KEEP
    positions = jnp.arange(BLOCK, dtype=jnp.int32)
    causal = positions[None, :] <= positions[:, None]

    def per_host(inputs):
        query_host, key_host, value_host, host = inputs
        all_keys = jnp.concatenate([key_blocks[0], passing_keys, key_host], axis=1)
        all_values = jnp.concatenate([value_blocks[0], passing_values, value_host], axis=1)
        anchor_seen = jnp.broadcast_to(host > 0, (BLOCK, BLOCK))
        passing_seen = jnp.broadcast_to(((owners >= 1) & (owners < host))[None, :], (BLOCK, hosts * KEEP))
        visible = jnp.concatenate([anchor_seen, passing_seen, causal], axis=1)
        scores = jnp.einsum('bgjd,gkd->gjbk', query_host.astype(jnp.float32), all_keys.astype(jnp.float32)) * scale_factor
        scores = jnp.where(visible[None, None], scores, -jnp.inf)
        row_top = lax.optimization_barrier(jnp.max(scores, axis=-1, keepdims=True))
        weights = jnp.exp(scores - row_top)
        total = lax.optimization_barrier(jnp.sum(weights, axis=-1))
        rounded = lax.optimization_barrier(weights.astype(jnp.bfloat16))
        summed = jnp.einsum('gjbk,gkd->bgjd', rounded.astype(jnp.float32), all_values.astype(jnp.float32))
        result = summed / total.transpose(2, 0, 1)[..., None]
        return result.astype(jnp.bfloat16).reshape(BLOCK, KVH * GROUP * HD)
    outputs = lax.map(per_host, (query_blocks, key_blocks, value_blocks, jnp.arange(hosts, dtype=jnp.int32)))
    return outputs.reshape(TOKENS, KVH * GROUP * HD)
```

```python
import functools
import math

import jax
import jax.numpy as jnp
from jax import lax
from jax.experimental import pallas as pl
from jax.experimental.pallas import tpu as pltpu
from jax.sharding import PartitionSpec as P

MESH = pl.DeviceIdType.MESH
heads_per_step = 2


def kernel(
    n, tps, far, q_hbm, k_hbm, v_hbm, pick_hbm, out,
    q, kv, kept, picks, local_scores, stage,
    load_sem, kv_send, kv_recv, out_send, out_recv, own_sem,
):
    rows, width = q_hbm.shape
    hd = k_hbm.shape[1]
    keep = picks.shape[2]
    group = width // hd
    part = rows // tps
    steps = group // heads_per_step
    h = lax.axis_index("ctx")
    t = lax.axis_index("tp")
    scale = math.log2(math.e) / math.sqrt(hd)

    loads = [
        pltpu.make_async_copy(k_hbm, kv.at[pl.ds(far, rows), pl.ds(0, hd)], load_sem.at[0]),
        pltpu.make_async_copy(v_hbm, kv.at[pl.ds(far, rows), pl.ds(hd, hd)], load_sem.at[1]),
        pltpu.make_async_copy(pick_hbm, picks, load_sem.at[2]),
        pltpu.make_async_copy(q_hbm, q, load_sem.at[3]),
    ]
    for load in loads:
        load.start()
    kv[0:far, 0 : 2 * hd] = jnp.zeros((far, 2 * hd), kv.dtype)
    kv[:, 2 * hd :] = jnp.ones((far + rows, hd), kv.dtype)

    barrier = pltpu.get_barrier_semaphore()

    def greet(j, carry):
        pl.semaphore_signal(barrier, inc=1, device_id={"ctx": j}, device_id_type=MESH)
        return carry

    lax.fori_loop(0, h, greet, 0)
    for d in range(1, tps):
        pl.semaphore_signal(
            barrier, inc=1, device_id={"tp": lax.rem(t + d, tps)}, device_id_type=MESH
        )

    loads[0].wait()
    loads[1].wait()
    loads[2].wait()
    hit = lax.broadcasted_iota(jnp.int32, (rows, keep), 0) == picks[0]
    kept[...] = lax.dot_general(
        hit.astype(jnp.float32).astype(jnp.bfloat16),
        kv[far:, 0 : 2 * hd],
        (((0,), (0,)), ((), ())),
        preferred_element_type=jnp.float32,
    ).astype(kept.dtype)

    pl.semaphore_wait(barrier, (n - 1 - h) + (tps - 1))

    def anchor_copy(j):
        return pltpu.make_async_remote_copy(
            src_ref=kv.at[pl.ds(far, rows), pl.ds(0, 2 * hd)],
            dst_ref=kv.at[pl.ds(0, rows), pl.ds(0, 2 * hd)],
            send_sem=kv_send.at[j],
            recv_sem=kv_recv.at[0],
            device_id={"ctx": j},
            device_id_type=MESH,
        )

    def kept_copy(owner, j):
        return pltpu.make_async_remote_copy(
            src_ref=kept,
            dst_ref=kv.at[pl.ds(rows + keep * (owner - 1), keep), pl.ds(0, 2 * hd)],
            send_sem=kv_send.at[j],
            recv_sem=kv_recv.at[owner],
            device_id={"ctx": j},
            device_id_type=MESH,
        )

    @pl.when(h == 0)
    def _():
        def go(i, carry):
            anchor_copy(n - i).start()
            return carry

        lax.fori_loop(1, n, go, 0)

    @pl.when(h > 0)
    def _():
        def go(j, carry):
            kept_copy(h, j).start()
            return carry

        lax.fori_loop(h + 1, n, go, 0)

    loads[3].wait()
    high = heads_per_step * rows
    causal = lax.broadcasted_iota(jnp.int32, (rows, rows), 1) <= lax.broadcasted_iota(
        jnp.int32, (rows, rows), 0
    )
    near = jnp.where(causal, 0.0, -jnp.inf)
    near = jnp.concatenate([near] * heads_per_step, axis=0)

    def head_rows(step):
        return jnp.concatenate(
            [
                q[:, (step * heads_per_step + i) * hd : (step * heads_per_step + i + 1) * hd]
                for i in range(heads_per_step)
            ],
            axis=0,
        )

    contract = (((1,), (1,)), ((), ()))
    for step in range(steps):
        local_scores[step * high : (step + 1) * high, :] = (
            lax.dot_general(
                head_rows(step), kv[far:, 0:hd], contract, preferred_element_type=jnp.float32
            )
            + near
        )

    @pl.when(h > 0)
    def _():
        anchor_copy(0).wait_recv()

        def arrive(j, carry):
            kept_copy(j, 0).wait_recv()
            return carry

        lax.fori_loop(1, h, arrive, 0)

    limit = jnp.where(h > 0, rows + keep * (h - 1), 0)
    bias = jnp.where(lax.broadcasted_iota(jnp.int32, (1, far), 1) < limit, 0.0, -jnp.inf)

    def out_copy(step, target, source):
        wide = heads_per_step * hd
        return pltpu.make_async_remote_copy(
            src_ref=stage.at[pl.ds(pl.multiple_of(target * part, part), part), pl.ds(step * wide, wide)],
            dst_ref=out.at[:, pl.ds(pl.multiple_of(source * width + step * wide, wide), wide)],
            send_sem=out_send.at[target, step],
            recv_sem=out_recv.at[source, step],
            device_id={"tp": target},
            device_id_type=MESH,
        )

    def own_copy(step):
        wide = heads_per_step * hd
        return pltpu.make_async_copy(
            stage.at[pl.ds(pl.multiple_of(t * part, part), part), pl.ds(step * wide, wide)],
            out.at[:, pl.ds(pl.multiple_of(t * width + step * wide, wide), wide)],
            own_sem.at[step],
        )

    for step in range(steps):
        scores = (
            lax.dot_general(
                head_rows(step), kv[0:far, 0:hd], contract, preferred_element_type=jnp.float32
            )
            + bias
        )
        own = local_scores[step * high : (step + 1) * high, :]
        top = jnp.maximum(
            jnp.max(scores, axis=1, keepdims=True), jnp.max(own, axis=1, keepdims=True)
        )
        weights = jnp.concatenate(
            [
                jnp.exp2((scores - top) * scale).astype(jnp.bfloat16),
                jnp.exp2((own - top) * scale).astype(jnp.bfloat16),
            ],
            axis=1,
        )
        summed = jnp.dot(weights, kv[:, hd:], preferred_element_type=jnp.float32)
        result = (summed[:, 0:hd] / summed[:, hd:]).astype(stage.dtype)
        for i in range(heads_per_step):
            head = step * heads_per_step + i
            stage[:, head * hd : (head + 1) * hd] = result[i * rows : (i + 1) * rows]
        for d in range(1, tps):
            out_copy(step, lax.rem(t + d, tps), t).start()
        own_copy(step).start()

    for step in range(steps):
        own_copy(step).wait()
        for d in range(1, tps):
            other = lax.rem(t + d, tps)
            out_copy(step, other, t).wait_send()
            out_copy(step, other, other).wait_recv()

    @pl.when(h == 0)
    def _():
        def done(i, carry):
            anchor_copy(n - i).wait_send()
            return carry

        lax.fori_loop(1, n, done, 0)

    @pl.when(h > 0)
    def _():
        def done(j, carry):
            kept_copy(h, j).wait_send()
            return carry

        lax.fori_loop(h + 1, n, done, 0)


def shards(n, tps, queries, key_rows, value_rows, retained):
    rows, width = queries.shape
    hd = key_rows.shape[1]
    keep = retained.shape[2]
    steps = width // hd // heads_per_step
    far = rows + -(-(n - 2) * keep // hd) * hd
    any_spec = pl.BlockSpec(memory_space=pl.ANY)
    return pl.pallas_call(
        functools.partial(kernel, n, tps, far),
        out_shape=jax.ShapeDtypeStruct((rows // tps, width * tps), queries.dtype),
        in_specs=[any_spec] * 4,
        out_specs=any_spec,
        scratch_shapes=[
            pltpu.VMEM((rows, width), jnp.bfloat16),
            pltpu.VMEM((far + rows, 3 * hd), jnp.bfloat16),
            pltpu.VMEM((keep, 2 * hd), jnp.bfloat16),
            pltpu.VMEM((1, 1, keep), jnp.int32),
            pltpu.VMEM((width // hd * rows, rows), jnp.float32),
            pltpu.VMEM((rows, width), jnp.bfloat16),
            pltpu.SemaphoreType.DMA((4,)),
            pltpu.SemaphoreType.DMA((n,)),
            pltpu.SemaphoreType.DMA((n,)),
            pltpu.SemaphoreType.DMA((tps, steps)),
            pltpu.SemaphoreType.DMA((tps, steps)),
            pltpu.SemaphoreType.DMA((steps,)),
        ],
        compiler_params=pltpu.CompilerParams(
            collective_id=0, has_side_effects=True, vmem_limit_bytes=48 * 1024 * 1024
        ),
        cost_estimate=pl.CostEstimate(
            flops=4 * width * rows * (far + rows),
            bytes_accessed=4 * rows * width,
            transcendentals=width // hd * rows * (far + rows),
        ),
    )(queries, key_rows, value_rows, retained)


def solution(mesh):
    in_specs = (P("ctx", "tp"), P("ctx", "tp"), P("ctx", "tp"), P("ctx", "tp", None))
    out_specs = P(("ctx", "tp"), None)
    return jax.shard_map(
        functools.partial(shards, mesh.shape["ctx"], mesh.shape["tp"]),
        mesh=mesh, in_specs=in_specs, out_specs=out_specs, check_vma=False,
    )
```

```python
import functools
import math

import jax
import jax.numpy as jnp
from jax import lax
from jax.experimental import pallas as pl
from jax.experimental.pallas import tpu as pltpu
from jax.sharding import PartitionSpec as P

MESH = pl.DeviceIdType.MESH
piece_rows = 16
turn_rows = 32


def kernel(
    n, tps, far, turn, q_hbm, k_hbm, v_hbm, pick_hbm, out,
    q, kv, kept, picks, local_scores, stage,
    load_sem, kv_send, kept_recv, piece_send, piece_recv, out_send, out_recv, own_sem,
):
    rows, width = q_hbm.shape
    hd = k_hbm.shape[1]
    keep = picks.shape[2]
    group = width // hd
    part = rows // tps
    subs = part // turn
    pieces = rows // piece_rows
    first_relay = n - pieces
    h = lax.axis_index("ctx")
    t = lax.axis_index("tp")
    scale = math.log2(math.e) / math.sqrt(hd)

    loads = [
        pltpu.make_async_copy(k_hbm, kv.at[pl.ds(far, rows), pl.ds(0, hd)], load_sem.at[0]),
        pltpu.make_async_copy(v_hbm, kv.at[pl.ds(far, rows), pl.ds(hd, hd)], load_sem.at[1]),
        pltpu.make_async_copy(pick_hbm, picks, load_sem.at[2]),
        pltpu.make_async_copy(q_hbm, q, load_sem.at[3]),
    ]
    for load in loads:
        load.start()
    kv[0:far, 0 : 2 * hd] = jnp.zeros((far, 2 * hd), kv.dtype)
    kv[:, 2 * hd :] = jnp.ones((far + rows, hd), kv.dtype)

    barrier = pltpu.get_barrier_semaphore()

    def greet(j, carry):
        pl.semaphore_signal(barrier, inc=1, device_id={"ctx": j}, device_id_type=MESH)
        return carry

    relay = h >= first_relay

    @pl.when(h > 0)
    def _():
        lax.fori_loop(jnp.where(relay, 0, 1), h, greet, 0)
        lax.fori_loop(jnp.maximum(h + 1, first_relay), n, greet, 0)

    for d in range(1, tps):
        pl.semaphore_signal(
            barrier, inc=1, device_id={"tp": lax.rem(t + d, tps)}, device_id_type=MESH
        )

    def scatter_copy(p):
        return pltpu.make_async_remote_copy(
            src_ref=kv.at[pl.ds(far + p * piece_rows, piece_rows), pl.ds(0, 2 * hd)],
            dst_ref=kv.at[pl.ds(p * piece_rows, piece_rows), pl.ds(0, 2 * hd)],
            send_sem=piece_send.at[p],
            recv_sem=piece_recv.at[p],
            device_id={"ctx": first_relay + p},
            device_id_type=MESH,
        )

    def piece_copy(p, j):
        return pltpu.make_async_remote_copy(
            src_ref=kv.at[pl.ds(p * piece_rows, piece_rows), pl.ds(0, 2 * hd)],
            dst_ref=kv.at[pl.ds(p * piece_rows, piece_rows), pl.ds(0, 2 * hd)],
            send_sem=piece_send.at[j],
            recv_sem=piece_recv.at[p],
            device_id={"ctx": j},
            device_id_type=MESH,
        )

    def kept_copy(owner, j):
        return pltpu.make_async_remote_copy(
            src_ref=kept,
            dst_ref=kv.at[pl.ds(rows + keep * (owner - 1), keep), pl.ds(0, 2 * hd)],
            send_sem=kv_send.at[j],
            recv_sem=kept_recv.at[owner],
            device_id={"ctx": j},
            device_id_type=MESH,
        )

    def loop(low, high, act):
        def body(j, carry):
            act(j)
            return carry

        lax.fori_loop(low, high, body, 0)

    loads[0].wait()
    loads[1].wait()
    reached = jnp.where(h == 0, pieces, jnp.where(relay, n - 2, n - 1 - h))
    pl.semaphore_wait(barrier, reached + (tps - 1))

    @pl.when(h == 0)
    def _():
        loop(0, pieces, lambda p: scatter_copy(p).start())

    loads[2].wait()
    hit = lax.broadcasted_iota(jnp.int32, (rows, keep), 0) == picks[0]
    kept[...] = lax.dot_general(
        hit.astype(jnp.float32).astype(jnp.bfloat16),
        kv[far:, 0 : 2 * hd],
        (((0,), (0,)), ((), ())),
        preferred_element_type=jnp.float32,
    ).astype(kept.dtype)

    @pl.when(h > 0)
    def _():
        loop(h + 1, n, lambda j: kept_copy(h, j).start())

    @pl.when(relay)
    def _():
        p = h - first_relay
        piece_copy(p, 0).wait_recv()
        loop(h + 1, n, lambda j: piece_copy(p, j).start())
        loop(1, h, lambda j: piece_copy(p, j).start())

    loads[3].wait()
    tall = group * turn
    contract = (((1,), (1,)), ((), ()))
    row_of = jnp.concatenate([lax.broadcasted_iota(jnp.int32, (turn, rows), 0)] * group, axis=0)
    column = lax.broadcasted_iota(jnp.int32, (tall, rows), 1)

    order = [(d % tps, sub) for d in range(1, tps + 1) for sub in range(subs)]

    def begin(step):
        d, sub = order[step]
        return pl.multiple_of(lax.rem(t + d, tps) * part + sub * turn, turn)

    def head_rows(step):
        return jnp.concatenate(
            [q[pl.ds(begin(step), turn), i * hd : (i + 1) * hd] for i in range(group)], axis=0
        )

    for step in range(len(order)):
        local_scores[step * tall : (step + 1) * tall, :] = jnp.where(
            column <= row_of + begin(step),
            lax.dot_general(
                head_rows(step), kv[far:, 0:hd], contract, preferred_element_type=jnp.float32
            ),
            -jnp.inf,
        )

    @pl.when(h > 0)
    def _():
        loop(1, h, lambda j: kept_copy(j, 0).wait_recv())

        def arrive(p):
            @pl.when(h != first_relay + p)
            def _():
                piece_copy(p, 0).wait_recv()

        loop(0, pieces, arrive)

    limit = jnp.where(h > 0, rows + keep * (h - 1), 0)
    bias = jnp.where(lax.broadcasted_iota(jnp.int32, (1, far), 1) < limit, 0.0, -jnp.inf)

    def out_copy(step, target, source):
        sub = order[step][1]
        return pltpu.make_async_remote_copy(
            src_ref=stage.at[pl.ds(begin(step), turn), :],
            dst_ref=out.at[pl.ds(sub * turn, turn), pl.ds(pl.multiple_of(source * width, width), width)],
            send_sem=out_send.at[step],
            recv_sem=out_recv.at[source, sub],
            device_id={"tp": target},
            device_id_type=MESH,
        )

    def own_copy(step):
        sub = order[step][1]
        return pltpu.make_async_copy(
            stage.at[pl.ds(begin(step), turn), :],
            out.at[pl.ds(sub * turn, turn), pl.ds(pl.multiple_of(t * width, width), width)],
            own_sem.at[sub],
        )

    for step in range(len(order)):
        scores = (
            lax.dot_general(
                head_rows(step), kv[0:far, 0:hd], contract, preferred_element_type=jnp.float32
            )
            + bias
        )
        own = local_scores[step * tall : (step + 1) * tall, :]
        top = jnp.maximum(
            jnp.max(scores, axis=1, keepdims=True), jnp.max(own, axis=1, keepdims=True)
        )
        weights = jnp.concatenate(
            [
                jnp.exp2((scores - top) * scale).astype(jnp.bfloat16),
                jnp.exp2((own - top) * scale).astype(jnp.bfloat16),
            ],
            axis=1,
        )
        summed = jnp.dot(weights, kv[:, hd:], preferred_element_type=jnp.float32)
        result = (summed[:, 0:hd] / summed[:, hd:]).astype(stage.dtype)
        for i in range(group):
            stage[pl.ds(begin(step), turn), i * hd : (i + 1) * hd] = result[
                i * turn : (i + 1) * turn
            ]
        d = order[step][0]
        if d:
            out_copy(step, lax.rem(t + d, tps), t).start()
        else:
            own_copy(step).start()

    @pl.when(h == 0)
    def _():
        loop(0, pieces, lambda p: scatter_copy(p).wait_send())

    @pl.when(h > 0)
    def _():
        loop(h + 1, n, lambda j: kept_copy(h, j).wait_send())

    @pl.when(relay)
    def _():
        p = h - first_relay
        loop(h + 1, n, lambda j: piece_copy(p, j).wait_send())
        loop(1, h, lambda j: piece_copy(p, j).wait_send())

    for step in range(len(order)):
        d = order[step][0]
        if d:
            other = lax.rem(t + d, tps)
            out_copy(step, other, t).wait_send()
            out_copy(step, other, other).wait_recv()
        else:
            own_copy(step).wait()


def shards(n, tps, queries, key_rows, value_rows, retained):
    rows, width = queries.shape
    hd = key_rows.shape[1]
    keep = retained.shape[2]
    part = rows // tps
    turn = min(turn_rows, part)
    subs = part // turn
    far = rows + -(-(n - 2) * keep // hd) * hd
    any_spec = pl.BlockSpec(memory_space=pl.ANY)
    return pl.pallas_call(
        functools.partial(kernel, n, tps, far, turn),
        out_shape=jax.ShapeDtypeStruct((rows // tps, width * tps), queries.dtype),
        in_specs=[any_spec] * 4,
        out_specs=any_spec,
        scratch_shapes=[
            pltpu.VMEM((rows, width), jnp.bfloat16),
            pltpu.VMEM((far + rows, 3 * hd), jnp.bfloat16),
            pltpu.VMEM((keep, 2 * hd), jnp.bfloat16),
            pltpu.VMEM((1, 1, keep), jnp.int32),
            pltpu.VMEM((width // hd * rows, rows), jnp.float32),
            pltpu.VMEM((rows, width), jnp.bfloat16),
            pltpu.SemaphoreType.DMA((4,)),
            pltpu.SemaphoreType.DMA((n,)),
            pltpu.SemaphoreType.DMA((n,)),
            pltpu.SemaphoreType.DMA((n,)),
            pltpu.SemaphoreType.DMA((rows // piece_rows,)),
            pltpu.SemaphoreType.DMA((tps * subs,)),
            pltpu.SemaphoreType.DMA((tps, subs)),
            pltpu.SemaphoreType.DMA((subs,)),
        ],
        compiler_params=pltpu.CompilerParams(
            collective_id=0, has_side_effects=True, vmem_limit_bytes=63 * 1024 * 1024
        ),
        cost_estimate=pl.CostEstimate(
            flops=4 * width * rows * (far + rows),
            bytes_accessed=4 * rows * width,
            transcendentals=width // hd * rows * (far + rows),
        ),
    )(queries, key_rows, value_rows, retained)


def solution(mesh):
    in_specs = (P("ctx", "tp"), P("ctx", "tp"), P("ctx", "tp"), P("ctx", "tp", None))
    out_specs = P(("ctx", "tp"), None)
    return jax.shard_map(
        functools.partial(shards, mesh.shape["ctx"], mesh.shape["tp"]),
        mesh=mesh, in_specs=in_specs, out_specs=out_specs, check_vma=False,
    )
```

```python
import functools
import math

import jax
import jax.numpy as jnp
from jax import lax
from jax.experimental import pallas as pl
from jax.experimental.pallas import tpu as pltpu
from jax.sharding import PartitionSpec as P

MESH = pl.DeviceIdType.MESH
turn_rows = 32


def kernel(
    n, tps, far, turn, q_hbm, k_hbm, v_hbm, pick_hbm, out,
    q, kv, kept, picks, local_scores, stage,
    load_sem, ready, kept_send, kept_recv, half_send, half_recv, out_send, out_recv, own_sem,
):
    rows, width = q_hbm.shape
    hd = k_hbm.shape[1]
    keep = picks.shape[2]
    group = width // hd
    part = rows // tps
    subs = part // turn
    half = rows // 2
    h = lax.axis_index("ctx")
    t = lax.axis_index("tp")
    scale = math.log2(math.e) / math.sqrt(hd)

    loads = [
        pltpu.make_async_copy(k_hbm, kv.at[pl.ds(far, rows), pl.ds(0, hd)], load_sem.at[0]),
        pltpu.make_async_copy(v_hbm, kv.at[pl.ds(far, rows), pl.ds(hd, hd)], load_sem.at[1]),
        pltpu.make_async_copy(pick_hbm, picks, load_sem.at[2]),
        pltpu.make_async_copy(q_hbm, q, load_sem.at[3]),
    ]
    for load in loads:
        load.start()
    kv[0:far, 0 : 2 * hd] = jnp.zeros((far, 2 * hd), kv.dtype)
    kv[:, 2 * hd :] = jnp.ones((far + rows, hd), kv.dtype)

    barrier = pltpu.get_barrier_semaphore()

    def loop(low, high, act):
        def body(j, carry):
            act(j)
            return carry

        lax.fori_loop(low, high, body, 0)

    def greet(j):
        pl.semaphore_signal(barrier, inc=1, device_id={"ctx": j}, device_id_type=MESH)

    for d in range(1, tps):
        pl.semaphore_signal(
            barrier, inc=1, device_id={"tp": lax.rem(t + d, tps)}, device_id_type=MESH
        )
    loop(h + 1, n, greet)

    def half_copy(side, base, j):
        return pltpu.make_async_remote_copy(
            src_ref=kv.at[pl.ds(base + side * half, half), pl.ds(0, 2 * hd)],
            dst_ref=kv.at[pl.ds(side * half, half), pl.ds(0, 2 * hd)],
            send_sem=half_send.at[j],
            recv_sem=half_recv.at[side],
            device_id={"ctx": j},
            device_id_type=MESH,
        )

    def second_half():
        return pltpu.make_async_remote_copy(
            src_ref=kv.at[pl.ds(far + half, half), pl.ds(0, 2 * hd)],
            dst_ref=kv.at[pl.ds(half, half), pl.ds(0, 2 * hd)],
            send_sem=half_send.at[0],
            recv_sem=half_recv.at[1],
            device_id={"ctx": 1},
            device_id_type=MESH,
        )

    def kept_copy(owner, j):
        return pltpu.make_async_remote_copy(
            src_ref=kept,
            dst_ref=kv.at[pl.ds(rows + keep * (owner - 1), keep), pl.ds(0, 2 * hd)],
            send_sem=kept_send.at[j],
            recv_sem=kept_recv.at[owner],
            device_id={"ctx": j},
            device_id_type=MESH,
        )

    loads[0].wait()
    loads[1].wait()
    loads[2].wait()
    hit = lax.broadcasted_iota(jnp.int32, (rows, keep), 0) == picks[0]
    kept[...] = lax.dot_general(
        hit.astype(jnp.float32).astype(jnp.bfloat16),
        kv[far:, 0 : 2 * hd],
        (((0,), (0,)), ((), ())),
        preferred_element_type=jnp.float32,
    ).astype(kept.dtype)

    pl.semaphore_wait(barrier, h + (tps - 1))

    def tell(j):
        pl.semaphore_signal(ready.at[h], inc=1, device_id={"ctx": j}, device_id_type=MESH)

    loop(0, h, tell)

    @pl.when(h == 0)
    def _():
        def serve(j):
            pl.semaphore_wait(ready.at[j], 1)

            @pl.when(j == 1)
            def _():
                second_half().start()

            @pl.when((j == 1) | (lax.rem(j, 2) == 0))
            def _():
                half_copy(0, far, j).start()

        loop(1, n, serve)

    @pl.when(h == 1)
    def _():
        half_copy(1, 0, 0).wait_recv()

        def serve(j):
            pl.semaphore_wait(ready.at[j], 1)

            @pl.when(lax.rem(j, 2) == 1)
            def _():
                half_copy(1, 0, j).start()

            kept_copy(1, j).start()

        loop(2, n, serve)
        half_copy(0, 0, 0).wait_recv()

    @pl.when(h > 1)
    def _():
        def serve(j):
            pl.semaphore_wait(ready.at[j], 1)
            kept_copy(h, j).start()

        loop(h + 1, n, serve)

        @pl.when(lax.rem(h, 2) == 0)
        def _():
            half_copy(0, 0, 0).wait_recv()
            half_copy(0, 0, h + 1).start()

        @pl.when(lax.rem(h, 2) == 1)
        def _():
            half_copy(1, 0, 0).wait_recv()
            half_copy(1, 0, h - 1).start()

    loads[3].wait()
    tall = group * turn
    contract = (((1,), (1,)), ((), ()))
    row_of = jnp.concatenate([lax.broadcasted_iota(jnp.int32, (turn, rows), 0)] * group, axis=0)
    column = lax.broadcasted_iota(jnp.int32, (tall, rows), 1)

    order = [(d % tps, sub) for d in range(1, tps + 1) for sub in range(subs)]

    def begin(step):
        d, sub = order[step]
        return pl.multiple_of(lax.rem(t + d, tps) * part + sub * turn, turn)

    def head_rows(step):
        return jnp.concatenate(
            [q[pl.ds(begin(step), turn), i * hd : (i + 1) * hd] for i in range(group)], axis=0
        )

    for step in range(len(order)):
        local_scores[step * tall : (step + 1) * tall, :] = jnp.where(
            column <= row_of + begin(step),
            lax.dot_general(
                head_rows(step), kv[far:, 0:hd], contract, preferred_element_type=jnp.float32
            ),
            -jnp.inf,
        )

    loop(1, h, lambda j: kept_copy(j, 0).wait_recv())

    @pl.when(h > 1)
    def _():
        @pl.when(lax.rem(h, 2) == 0)
        def _():
            half_copy(1, 0, 0).wait_recv()

        @pl.when(lax.rem(h, 2) == 1)
        def _():
            half_copy(0, 0, 0).wait_recv()

    limit = jnp.where(h > 0, rows + keep * (h - 1), 0)
    bias = jnp.where(lax.broadcasted_iota(jnp.int32, (1, far), 1) < limit, 0.0, -jnp.inf)

    def out_copy(step, target, source):
        sub = order[step][1]
        return pltpu.make_async_remote_copy(
            src_ref=stage.at[pl.ds(begin(step), turn), :],
            dst_ref=out.at[pl.ds(sub * turn, turn), pl.ds(pl.multiple_of(source * width, width), width)],
            send_sem=out_send.at[step],
            recv_sem=out_recv.at[source, sub],
            device_id={"tp": target},
            device_id_type=MESH,
        )

    def own_copy(step):
        sub = order[step][1]
        return pltpu.make_async_copy(
            stage.at[pl.ds(begin(step), turn), :],
            out.at[pl.ds(sub * turn, turn), pl.ds(pl.multiple_of(t * width, width), width)],
            own_sem.at[sub],
        )

    for step in range(len(order)):
        scores = (
            lax.dot_general(
                head_rows(step), kv[0:far, 0:hd], contract, preferred_element_type=jnp.float32
            )
            + bias
        )
        own = local_scores[step * tall : (step + 1) * tall, :]
        top = jnp.maximum(
            jnp.max(scores, axis=1, keepdims=True), jnp.max(own, axis=1, keepdims=True)
        )
        weights = jnp.concatenate(
            [
                jnp.exp2((scores - top) * scale).astype(jnp.bfloat16),
                jnp.exp2((own - top) * scale).astype(jnp.bfloat16),
            ],
            axis=1,
        )
        summed = jnp.dot(weights, kv[:, hd:], preferred_element_type=jnp.float32)
        result = (summed[:, 0:hd] / summed[:, hd:]).astype(stage.dtype)
        for i in range(group):
            stage[pl.ds(begin(step), turn), i * hd : (i + 1) * hd] = result[
                i * turn : (i + 1) * turn
            ]
        d = order[step][0]
        if d:
            out_copy(step, lax.rem(t + d, tps), t).start()
        else:
            own_copy(step).start()

    @pl.when(h == 0)
    def _():
        second_half().wait_send()
        half_copy(0, far, 1).wait_send()
        loop(1, n // 2, lambda i: half_copy(0, far, 2 * i).wait_send())

    @pl.when(h == 1)
    def _():
        loop(1, n // 2, lambda i: half_copy(1, 0, 2 * i + 1).wait_send())

    @pl.when(h > 0)
    def _():
        loop(h + 1, n, lambda j: kept_copy(h, j).wait_send())

    @pl.when((h > 1) & (lax.rem(h, 2) == 0))
    def _():
        half_copy(0, 0, h + 1).wait_send()

    @pl.when((h > 1) & (lax.rem(h, 2) == 1))
    def _():
        half_copy(1, 0, h - 1).wait_send()

    for step in range(len(order)):
        d = order[step][0]
        if d:
            other = lax.rem(t + d, tps)
            out_copy(step, other, t).wait_send()
            out_copy(step, other, other).wait_recv()
        else:
            own_copy(step).wait()


def shards(n, tps, queries, key_rows, value_rows, retained):
    rows, width = queries.shape
    hd = key_rows.shape[1]
    keep = retained.shape[2]
    part = rows // tps
    turn = min(turn_rows, part)
    subs = part // turn
    far = rows + -(-(n - 2) * keep // hd) * hd
    any_spec = pl.BlockSpec(memory_space=pl.ANY)
    return pl.pallas_call(
        functools.partial(kernel, n, tps, far, turn),
        out_shape=jax.ShapeDtypeStruct((rows // tps, width * tps), queries.dtype),
        in_specs=[any_spec] * 4,
        out_specs=any_spec,
        scratch_shapes=[
            pltpu.VMEM((rows, width), jnp.bfloat16),
            pltpu.VMEM((far + rows, 3 * hd), jnp.bfloat16),
            pltpu.VMEM((keep, 2 * hd), jnp.bfloat16),
            pltpu.VMEM((1, 1, keep), jnp.int32),
            pltpu.VMEM((width // hd * rows, rows), jnp.float32),
            pltpu.VMEM((rows, width), jnp.bfloat16),
            pltpu.SemaphoreType.DMA((4,)),
            pltpu.SemaphoreType.REGULAR((n,)),
            pltpu.SemaphoreType.DMA((n,)),
            pltpu.SemaphoreType.DMA((n,)),
            pltpu.SemaphoreType.DMA((n,)),
            pltpu.SemaphoreType.DMA((2,)),
            pltpu.SemaphoreType.DMA((tps * subs,)),
            pltpu.SemaphoreType.DMA((tps, subs)),
            pltpu.SemaphoreType.DMA((subs,)),
        ],
        compiler_params=pltpu.CompilerParams(
            collective_id=0, has_side_effects=True, vmem_limit_bytes=48 * 1024 * 1024
        ),
        cost_estimate=pl.CostEstimate(
            flops=4 * width * rows * (far + rows),
            bytes_accessed=4 * rows * width,
            transcendentals=width // hd * rows * (far + rows),
        ),
    )(*(pltpu.with_memory_space_constraint(x, pltpu.HBM) for x in (queries, key_rows, value_rows, retained)))


def solution(mesh):
    in_specs = (P("ctx", "tp"), P("ctx", "tp"), P("ctx", "tp"), P("ctx", "tp", None))
    out_specs = P(("ctx", "tp"), None)
    return jax.shard_map(
        functools.partial(shards, mesh.shape["ctx"], mesh.shape["tp"]),
        mesh=mesh, in_specs=in_specs, out_specs=out_specs, check_vma=False,
    )
```

```python
import functools
import math

import jax
import jax.numpy as jnp
from jax import lax
from jax.experimental import pallas as pl
from jax.experimental.pallas import tpu as pltpu
from jax.sharding import PartitionSpec as P

MESH = pl.DeviceIdType.MESH
turn_rows = 32


def kernel(
    n, tps, far, turn, q_hbm, k_hbm, v_hbm, pick_hbm, out,
    q, kv, kept, picks, local_scores, stage,
    load_sem, ready, forward_send, kept_send, kept_recv, half_send, half_recv, out_send, out_recv, own_sem,
):
    rows, width = q_hbm.shape
    hd = k_hbm.shape[1]
    keep = picks.shape[2]
    group = width // hd
    part = rows // tps
    subs = part // turn
    half = rows // 2
    chips = n // 2
    h = lax.axis_index("ctx")
    t = lax.axis_index("tp")
    c, p = h // 2, lax.rem(h, 2)
    mate = h + 1 - 2 * p
    scale = math.log2(math.e) / math.sqrt(hd)

    loads = [
        pltpu.make_async_copy(k_hbm, kv.at[pl.ds(far, rows), pl.ds(0, hd)], load_sem.at[0]),
        pltpu.make_async_copy(v_hbm, kv.at[pl.ds(far, rows), pl.ds(hd, hd)], load_sem.at[1]),
        pltpu.make_async_copy(pick_hbm, picks, load_sem.at[2]),
        pltpu.make_async_copy(q_hbm, q, load_sem.at[3]),
    ]
    for load in loads:
        load.start()
    kv[0:far, 0 : 2 * hd] = jnp.zeros((far, 2 * hd), kv.dtype)
    kv[:, 2 * hd :] = jnp.ones((far + rows, hd), kv.dtype)

    barrier = pltpu.get_barrier_semaphore()

    def loop(low, high, act):
        def body(j, carry):
            act(j)
            return carry

        lax.fori_loop(low, high, body, 0)

    def greet(j):
        pl.semaphore_signal(barrier, inc=1, device_id={"ctx": j}, device_id_type=MESH)

    for d in range(1, tps):
        pl.semaphore_signal(
            barrier, inc=1, device_id={"tp": lax.rem(t + d, tps)}, device_id_type=MESH
        )
    greet(mate)
    loop(c + 1, chips, lambda i: greet(2 * i + p))

    def half_copy(side, base, j):
        return pltpu.make_async_remote_copy(
            src_ref=kv.at[pl.ds(base + side * half, half), pl.ds(0, 2 * hd)],
            dst_ref=kv.at[pl.ds(side * half, half), pl.ds(0, 2 * hd)],
            send_sem=half_send.at[j],
            recv_sem=half_recv.at[side],
            device_id={"ctx": j},
            device_id_type=MESH,
        )

    def second_half():
        return pltpu.make_async_remote_copy(
            src_ref=kv.at[pl.ds(far + half, half), pl.ds(0, 2 * hd)],
            dst_ref=kv.at[pl.ds(half, half), pl.ds(0, 2 * hd)],
            send_sem=half_send.at[0],
            recv_sem=half_recv.at[1],
            device_id={"ctx": 1},
            device_id_type=MESH,
        )

    def kept_copy(owner, j):
        return pltpu.make_async_remote_copy(
            src_ref=kept,
            dst_ref=kv.at[pl.ds(rows + keep * (owner - 1), keep), pl.ds(0, 2 * hd)],
            send_sem=kept_send.at[j],
            recv_sem=kept_recv.at[owner],
            device_id={"ctx": j},
            device_id_type=MESH,
        )

    def forward_copy(owner):
        slot = kv.at[pl.ds(rows + keep * (owner - 1), keep), pl.ds(0, 2 * hd)]
        return pltpu.make_async_remote_copy(
            src_ref=slot,
            dst_ref=slot,
            send_sem=forward_send.at[owner],
            recv_sem=kept_recv.at[owner],
            device_id={"ctx": mate},
            device_id_type=MESH,
        )

    loads[0].wait()
    loads[1].wait()
    loads[2].wait()
    hit = lax.broadcasted_iota(jnp.int32, (rows, keep), 0) == picks[0]
    kept[...] = lax.dot_general(
        hit.astype(jnp.float32).astype(jnp.bfloat16),
        kv[far:, 0 : 2 * hd],
        (((0,), (0,)), ((), ())),
        preferred_element_type=jnp.float32,
    ).astype(kept.dtype)

    pl.semaphore_wait(barrier, c + tps)

    def tell(i):
        pl.semaphore_signal(ready.at[h], inc=1, device_id={"ctx": 2 * i + p}, device_id_type=MESH)

    loop(0, c, tell)

    @pl.when(h == 0)
    def _():
        second_half().start()

        def serve(i):
            pl.semaphore_wait(ready.at[2 * i], 1)
            half_copy(0, far, 2 * i).start()

        loop(1, 2, serve)
        half_copy(0, far, 1).start()
        loop(2, chips, serve)

    @pl.when(h == 1)
    def _():
        half_copy(1, 0, 0).wait_recv()

        def serve(i):
            pl.semaphore_wait(ready.at[2 * i + 1], 1)
            half_copy(1, 0, 2 * i + 1).start()
            kept_copy(1, 2 * i + 1).start()

        loop(1, chips, serve)
        half_copy(0, 0, 0).wait_recv()

    @pl.when(c > 0)
    def _():
        @pl.when(p == 0)
        def _():
            kept_copy(h, h + 1).start()

        def serve(i):
            pl.semaphore_wait(ready.at[2 * i + p], 1)
            kept_copy(h, 2 * i + p).start()

        loop(c + 1, chips, serve)
        half_copy(p, 0, 0).wait_recv()
        half_copy(p, 0, mate).start()

        def forward(i):
            owner = 2 * i + p
            forward_copy(owner).wait_recv()
            forward_copy(owner).start()

        loop(1 - p, c, forward)

    loads[3].wait()
    tall = group * turn
    contract = (((1,), (1,)), ((), ()))
    row_of = jnp.concatenate([lax.broadcasted_iota(jnp.int32, (turn, rows), 0)] * group, axis=0)
    column = lax.broadcasted_iota(jnp.int32, (tall, rows), 1)

    order = [(d % tps, sub) for d in range(1, tps + 1) for sub in range(subs)]

    def begin(step):
        d, sub = order[step]
        return pl.multiple_of(lax.rem(t + d, tps) * part + sub * turn, turn)

    def head_rows(step):
        return jnp.concatenate(
            [q[pl.ds(begin(step), turn), i * hd : (i + 1) * hd] for i in range(group)], axis=0
        )

    for step in range(len(order)):
        local_scores[step * tall : (step + 1) * tall, :] = jnp.where(
            column <= row_of + begin(step),
            lax.dot_general(
                head_rows(step), kv[far:, 0:hd], contract, preferred_element_type=jnp.float32
            ),
            -jnp.inf,
        )

    @pl.when(c > 0)
    def _():
        half_copy(1 - p, 0, 0).wait_recv()
        loop(p, c + p, lambda i: forward_copy(2 * i + 1 - p).wait_recv())

    limit = jnp.where(h > 0, rows + keep * (h - 1), 0)
    bias = jnp.where(lax.broadcasted_iota(jnp.int32, (1, far), 1) < limit, 0.0, -jnp.inf)

    def out_copy(step, target, source):
        sub = order[step][1]
        return pltpu.make_async_remote_copy(
            src_ref=stage.at[pl.ds(begin(step), turn), :],
            dst_ref=out.at[pl.ds(sub * turn, turn), pl.ds(pl.multiple_of(source * width, width), width)],
            send_sem=out_send.at[step],
            recv_sem=out_recv.at[source, sub],
            device_id={"tp": target},
            device_id_type=MESH,
        )

    def own_copy(step):
        sub = order[step][1]
        return pltpu.make_async_copy(
            stage.at[pl.ds(begin(step), turn), :],
            out.at[pl.ds(sub * turn, turn), pl.ds(pl.multiple_of(t * width, width), width)],
            own_sem.at[sub],
        )

    for step in range(len(order)):
        scores = (
            lax.dot_general(
                head_rows(step), kv[0:far, 0:hd], contract, preferred_element_type=jnp.float32
            )
            + bias
        )
        own = local_scores[step * tall : (step + 1) * tall, :]
        top = jnp.maximum(
            jnp.max(scores, axis=1, keepdims=True), jnp.max(own, axis=1, keepdims=True)
        )
        weights = jnp.concatenate(
            [
                jnp.exp2((scores - top) * scale).astype(jnp.bfloat16),
                jnp.exp2((own - top) * scale).astype(jnp.bfloat16),
            ],
            axis=1,
        )
        summed = jnp.dot(weights, kv[:, hd:], preferred_element_type=jnp.float32)
        result = (summed[:, 0:hd] / summed[:, hd:]).astype(stage.dtype)
        for i in range(group):
            stage[pl.ds(begin(step), turn), i * hd : (i + 1) * hd] = result[
                i * turn : (i + 1) * turn
            ]
        d = order[step][0]
        if d:
            out_copy(step, lax.rem(t + d, tps), t).start()
        else:
            own_copy(step).start()

    @pl.when(h == 0)
    def _():
        second_half().wait_send()
        half_copy(0, far, 1).wait_send()
        loop(1, chips, lambda i: half_copy(0, far, 2 * i).wait_send())

    @pl.when(h == 1)
    def _():
        loop(1, chips, lambda i: half_copy(1, 0, 2 * i + 1).wait_send())

    @pl.when(h > 0)
    def _():
        loop(c + 1, chips, lambda i: kept_copy(h, 2 * i + p).wait_send())

    @pl.when(c > 0)
    def _():
        @pl.when(p == 0)
        def _():
            kept_copy(h, h + 1).wait_send()

        half_copy(p, 0, mate).wait_send()
        loop(1 - p, c, lambda i: forward_copy(2 * i + p).wait_send())

    for step in range(len(order)):
        d = order[step][0]
        if d:
            other = lax.rem(t + d, tps)
            out_copy(step, other, t).wait_send()
            out_copy(step, other, other).wait_recv()
        else:
            own_copy(step).wait()


def shards(n, tps, queries, key_rows, value_rows, retained):
    rows, width = queries.shape
    hd = key_rows.shape[1]
    keep = retained.shape[2]
    part = rows // tps
    turn = min(turn_rows, part)
    subs = part // turn
    far = rows + -(-(n - 2) * keep // hd) * hd
    any_spec = pl.BlockSpec(memory_space=pl.ANY)
    return pl.pallas_call(
        functools.partial(kernel, n, tps, far, turn),
        out_shape=jax.ShapeDtypeStruct((rows // tps, width * tps), queries.dtype),
        in_specs=[any_spec] * 4,
        out_specs=any_spec,
        scratch_shapes=[
            pltpu.VMEM((rows, width), jnp.bfloat16),
            pltpu.VMEM((far + rows, 3 * hd), jnp.bfloat16),
            pltpu.VMEM((keep, 2 * hd), jnp.bfloat16),
            pltpu.VMEM((1, 1, keep), jnp.int32),
            pltpu.VMEM((width // hd * rows, rows), jnp.float32),
            pltpu.VMEM((rows, width), jnp.bfloat16),
            pltpu.SemaphoreType.DMA((4,)),
            pltpu.SemaphoreType.REGULAR((n,)),
            pltpu.SemaphoreType.DMA((n,)),
            pltpu.SemaphoreType.DMA((n,)),
            pltpu.SemaphoreType.DMA((n,)),
            pltpu.SemaphoreType.DMA((n,)),
            pltpu.SemaphoreType.DMA((2,)),
            pltpu.SemaphoreType.DMA((tps * subs,)),
            pltpu.SemaphoreType.DMA((tps, subs)),
            pltpu.SemaphoreType.DMA((subs,)),
        ],
        compiler_params=pltpu.CompilerParams(
            collective_id=0, has_side_effects=True, vmem_limit_bytes=48 * 1024 * 1024
        ),
        cost_estimate=pl.CostEstimate(
            flops=4 * width * rows * (far + rows),
            bytes_accessed=4 * rows * width,
            transcendentals=width // hd * rows * (far + rows),
        ),
    )(*(pltpu.with_memory_space_constraint(x, pltpu.HBM) for x in (queries, key_rows, value_rows, retained)))


def solution(mesh):
    in_specs = (P("ctx", "tp"), P("ctx", "tp"), P("ctx", "tp"), P("ctx", "tp", None))
    out_specs = P(("ctx", "tp"), None)
    return jax.shard_map(
        functools.partial(shards, mesh.shape["ctx"], mesh.shape["tp"]),
        mesh=mesh, in_specs=in_specs, out_specs=out_specs, check_vma=False,
    )
```

```python
import functools
import math

import jax
import jax.numpy as jnp
from jax import lax
from jax.experimental import pallas as pl
from jax.experimental.pallas import tpu as pltpu
from jax.sharding import PartitionSpec as P

MESH = pl.DeviceIdType.MESH
turn_rows = 32


def kernel(
    n, tps, far, turn, q_hbm, k_hbm, v_hbm, pick_hbm, out,
    q, kv, kept, picks, local_scores, stage,
    load_sem, forward_send, kept_send, kept_recv, half_send, half_recv, out_send, out_recv, own_sem,
):
    rows, width = q_hbm.shape
    hd = k_hbm.shape[1]
    keep = picks.shape[2]
    group = width // hd
    part = rows // tps
    subs = part // turn
    half = rows // 2
    chips = n // 2
    h = lax.axis_index("ctx")
    t = lax.axis_index("tp")
    c, p = h // 2, lax.rem(h, 2)
    mate = h + 1 - 2 * p
    scale = math.log2(math.e) / math.sqrt(hd)

    loads = [
        pltpu.make_async_copy(k_hbm, kv.at[pl.ds(far, rows), pl.ds(0, hd)], load_sem.at[0]),
        pltpu.make_async_copy(v_hbm, kv.at[pl.ds(far, rows), pl.ds(hd, hd)], load_sem.at[1]),
        pltpu.make_async_copy(pick_hbm, picks, load_sem.at[2]),
        pltpu.make_async_copy(q_hbm, q, load_sem.at[3]),
    ]
    for load in loads:
        load.start()
    kv[0:far, 0 : 2 * hd] = jnp.zeros((far, 2 * hd), kv.dtype)
    kv[:, 2 * hd :] = jnp.ones((far + rows, hd), kv.dtype)

    barrier = pltpu.get_barrier_semaphore()

    def loop(low, high, act):
        def body(j, carry):
            act(j)
            return carry

        lax.fori_loop(low, high, body, 0)

    def greet(j):
        pl.semaphore_signal(barrier, inc=1, device_id={"ctx": j}, device_id_type=MESH)

    for d in range(1, tps):
        pl.semaphore_signal(
            barrier, inc=1, device_id={"tp": lax.rem(t + d, tps)}, device_id_type=MESH
        )
    greet(mate)
    loop(0, c, lambda i: greet(2 * i + p))

    def half_copy(side, base, j):
        return pltpu.make_async_remote_copy(
            src_ref=kv.at[pl.ds(base + side * half, half), pl.ds(0, 2 * hd)],
            dst_ref=kv.at[pl.ds(side * half, half), pl.ds(0, 2 * hd)],
            send_sem=half_send.at[j],
            recv_sem=half_recv.at[side],
            device_id={"ctx": j},
            device_id_type=MESH,
        )

    def second_half():
        return pltpu.make_async_remote_copy(
            src_ref=kv.at[pl.ds(far + half, half), pl.ds(0, 2 * hd)],
            dst_ref=kv.at[pl.ds(half, half), pl.ds(0, 2 * hd)],
            send_sem=half_send.at[0],
            recv_sem=half_recv.at[1],
            device_id={"ctx": 1},
            device_id_type=MESH,
        )

    def kept_copy(owner, j):
        return pltpu.make_async_remote_copy(
            src_ref=kept,
            dst_ref=kv.at[pl.ds(rows + keep * (owner - 1), keep), pl.ds(0, 2 * hd)],
            send_sem=kept_send.at[j],
            recv_sem=kept_recv.at[owner],
            device_id={"ctx": j},
            device_id_type=MESH,
        )

    def forward_copy(owner):
        slot = kv.at[pl.ds(rows + keep * (owner - 1), keep), pl.ds(0, 2 * hd)]
        return pltpu.make_async_remote_copy(
            src_ref=slot,
            dst_ref=slot,
            send_sem=forward_send.at[owner],
            recv_sem=kept_recv.at[owner],
            device_id={"ctx": mate},
            device_id_type=MESH,
        )

    loads[0].wait()
    loads[1].wait()
    loads[2].wait()
    hit = lax.broadcasted_iota(jnp.int32, (rows, keep), 0) == picks[0]
    kept[...] = lax.dot_general(
        hit.astype(jnp.float32).astype(jnp.bfloat16),
        kv[far:, 0 : 2 * hd],
        (((0,), (0,)), ((), ())),
        preferred_element_type=jnp.float32,
    ).astype(kept.dtype)

    loads[3].wait()
    tall = group * turn
    contract = (((1,), (1,)), ((), ()))
    row_of = jnp.concatenate([lax.broadcasted_iota(jnp.int32, (turn, rows), 0)] * group, axis=0)
    column = lax.broadcasted_iota(jnp.int32, (tall, rows), 1)

    order = [(d % tps, sub) for d in range(1, tps + 1) for sub in range(subs)]

    def begin(step):
        d, sub = order[step]
        return pl.multiple_of(lax.rem(t + d, tps) * part + sub * turn, turn)

    def head_rows(step):
        return jnp.concatenate(
            [q[pl.ds(begin(step), turn), i * hd : (i + 1) * hd] for i in range(group)], axis=0
        )

    for step in range(len(order)):
        local_scores[step * tall : (step + 1) * tall, :] = jnp.where(
            column <= row_of + begin(step),
            lax.dot_general(
                head_rows(step), kv[far:, 0:hd], contract, preferred_element_type=jnp.float32
            ),
            -jnp.inf,
        )

    pl.semaphore_wait(barrier, chips - 1 - c + tps)

    @pl.when(h == 0)
    def _():
        second_half().start()

        def serve(i):
            half_copy(0, far, 2 * i).start()

        loop(1, 2, serve)
        half_copy(0, far, 1).start()
        loop(2, chips, serve)

    @pl.when(h == 1)
    def _():
        half_copy(1, 0, 0).wait_recv()

        def serve(i):
            half_copy(1, 0, 2 * i + 1).start()
            kept_copy(1, 2 * i + 1).start()

        loop(1, chips, serve)
        half_copy(0, 0, 0).wait_recv()

    @pl.when(c > 0)
    def _():
        @pl.when(p == 0)
        def _():
            kept_copy(h, h + 1).start()

        def serve(i):
            kept_copy(h, 2 * i + p).start()

        loop(c + 1, chips, serve)
        def forward(i):
            owner = 2 * i + p
            forward_copy(owner).wait_recv()
            forward_copy(owner).start()

        loop(1 - p, c, forward)
        half_copy(p, 0, 0).wait_recv()
        half_copy(p, 0, mate).start()

    @pl.when(c > 0)
    def _():
        half_copy(1 - p, 0, 0).wait_recv()
        loop(p, c + p, lambda i: forward_copy(2 * i + 1 - p).wait_recv())

    limit = jnp.where(h > 0, rows + keep * (h - 1), 0)
    bias = jnp.where(lax.broadcasted_iota(jnp.int32, (1, far), 1) < limit, 0.0, -jnp.inf)

    def out_copy(step, target, source):
        sub = order[step][1]
        return pltpu.make_async_remote_copy(
            src_ref=stage.at[pl.ds(begin(step), turn), :],
            dst_ref=out.at[pl.ds(sub * turn, turn), pl.ds(pl.multiple_of(source * width, width), width)],
            send_sem=out_send.at[step],
            recv_sem=out_recv.at[source, sub],
            device_id={"tp": target},
            device_id_type=MESH,
        )

    def own_copy(step):
        sub = order[step][1]
        return pltpu.make_async_copy(
            stage.at[pl.ds(begin(step), turn), :],
            out.at[pl.ds(sub * turn, turn), pl.ds(pl.multiple_of(t * width, width), width)],
            own_sem.at[sub],
        )

    for step in range(len(order)):
        scores = (
            lax.dot_general(
                head_rows(step), kv[0:far, 0:hd], contract, preferred_element_type=jnp.float32
            )
            + bias
        )
        own = local_scores[step * tall : (step + 1) * tall, :]
        top = jnp.maximum(
            jnp.max(scores, axis=1, keepdims=True), jnp.max(own, axis=1, keepdims=True)
        )
        weights = jnp.concatenate(
            [
                jnp.exp2((scores - top) * scale).astype(jnp.bfloat16),
                jnp.exp2((own - top) * scale).astype(jnp.bfloat16),
            ],
            axis=1,
        )
        summed = jnp.dot(weights, kv[:, hd:], preferred_element_type=jnp.float32)
        result = (summed[:, 0:hd] / summed[:, hd:]).astype(stage.dtype)
        for i in range(group):
            stage[pl.ds(begin(step), turn), i * hd : (i + 1) * hd] = result[
                i * turn : (i + 1) * turn
            ]
        d = order[step][0]
        if d:
            out_copy(step, lax.rem(t + d, tps), t).start()
        else:
            own_copy(step).start()

    @pl.when(h == 0)
    def _():
        second_half().wait_send()
        half_copy(0, far, 1).wait_send()
        loop(1, chips, lambda i: half_copy(0, far, 2 * i).wait_send())

    @pl.when(h == 1)
    def _():
        loop(1, chips, lambda i: half_copy(1, 0, 2 * i + 1).wait_send())

    @pl.when(h > 0)
    def _():
        loop(c + 1, chips, lambda i: kept_copy(h, 2 * i + p).wait_send())

    @pl.when(c > 0)
    def _():
        @pl.when(p == 0)
        def _():
            kept_copy(h, h + 1).wait_send()

        half_copy(p, 0, mate).wait_send()
        loop(1 - p, c, lambda i: forward_copy(2 * i + p).wait_send())

    for step in range(len(order)):
        d = order[step][0]
        if d:
            other = lax.rem(t + d, tps)
            out_copy(step, other, t).wait_send()
            out_copy(step, other, other).wait_recv()
        else:
            own_copy(step).wait()


def shards(n, tps, queries, key_rows, value_rows, retained):
    rows, width = queries.shape
    hd = key_rows.shape[1]
    keep = retained.shape[2]
    part = rows // tps
    turn = min(turn_rows, part)
    subs = part // turn
    far = rows + -(-(n - 2) * keep // hd) * hd
    any_spec = pl.BlockSpec(memory_space=pl.ANY)
    return pl.pallas_call(
        functools.partial(kernel, n, tps, far, turn),
        out_shape=jax.ShapeDtypeStruct((rows // tps, width * tps), queries.dtype),
        in_specs=[any_spec] * 4,
        out_specs=any_spec,
        scratch_shapes=[
            pltpu.VMEM((rows, width), jnp.bfloat16),
            pltpu.VMEM((far + rows, 3 * hd), jnp.bfloat16),
            pltpu.VMEM((keep, 2 * hd), jnp.bfloat16),
            pltpu.VMEM((1, 1, keep), jnp.int32),
            pltpu.VMEM((width // hd * rows, rows), jnp.float32),
            pltpu.VMEM((rows, width), jnp.bfloat16),
            pltpu.SemaphoreType.DMA((4,)),
            pltpu.SemaphoreType.DMA((n,)),
            pltpu.SemaphoreType.DMA((n,)),
            pltpu.SemaphoreType.DMA((n,)),
            pltpu.SemaphoreType.DMA((n,)),
            pltpu.SemaphoreType.DMA((2,)),
            pltpu.SemaphoreType.DMA((tps * subs,)),
            pltpu.SemaphoreType.DMA((tps, subs)),
            pltpu.SemaphoreType.DMA((subs,)),
        ],
        compiler_params=pltpu.CompilerParams(
            collective_id=0, has_side_effects=True, vmem_limit_bytes=48 * 1024 * 1024
        ),
        cost_estimate=pl.CostEstimate(
            flops=4 * width * rows * (far + rows),
            bytes_accessed=4 * rows * width,
            transcendentals=width // hd * rows * (far + rows),
        ),
    )(*(pltpu.with_memory_space_constraint(x, pltpu.HBM) for x in (queries, key_rows, value_rows, retained)))


def solution(mesh):
    in_specs = (P("ctx", "tp"), P("ctx", "tp"), P("ctx", "tp"), P("ctx", "tp", None))
    out_specs = P(("ctx", "tp"), None)
    return jax.shard_map(
        functools.partial(shards, mesh.shape["ctx"], mesh.shape["tp"]),
        mesh=mesh, in_specs=in_specs, out_specs=out_specs, check_vma=False,
    )
```

```python
import functools
import math

import jax
import jax.numpy as jnp
from jax import lax
from jax.experimental import pallas as pl
from jax.experimental.pallas import tpu as pltpu
from jax.sharding import PartitionSpec as P

MESH = pl.DeviceIdType.MESH
turn_rows = 32


def kernel(
    n, tps, far, turn, q_hbm, k_hbm, v_hbm, pick_hbm, out,
    q, kv, kept, picks, local_scores, stage,
    load_sem, ready, forward_send, kept_send, kept_recv, half_send, half_recv, out_send, out_recv, own_sem,
):
    rows, width = q_hbm.shape
    hd = k_hbm.shape[1]
    keep = picks.shape[2]
    group = width // hd
    part = rows // tps
    subs = part // turn
    half = rows // 2
    chips = n // 2
    h = lax.axis_index("ctx")
    t = lax.axis_index("tp")
    c, p = h // 2, lax.rem(h, 2)
    mate = h + 1 - 2 * p
    scale = math.log2(math.e) / math.sqrt(hd)

    barrier = pltpu.get_barrier_semaphore()

    def loop(low, high, act):
        def body(j, carry):
            act(j)
            return carry

        lax.fori_loop(low, high, body, 0)

    def greet(j):
        pl.semaphore_signal(barrier, inc=1, device_id={"ctx": j}, device_id_type=MESH)

    for d in range(1, tps):
        pl.semaphore_signal(
            barrier, inc=1, device_id={"tp": lax.rem(t + d, tps)}, device_id_type=MESH
        )
    loop(c + 1, chips, lambda i: greet(2 * i + p))

    loads = [
        pltpu.make_async_copy(k_hbm, kv.at[pl.ds(far, rows), pl.ds(0, hd)], load_sem.at[0]),
        pltpu.make_async_copy(v_hbm, kv.at[pl.ds(far, rows), pl.ds(hd, hd)], load_sem.at[1]),
        pltpu.make_async_copy(pick_hbm, picks, load_sem.at[2]),
        pltpu.make_async_copy(q_hbm, q, load_sem.at[3]),
    ]
    for load in loads:
        load.start()
    kv[0:far, 0 : 2 * hd] = jnp.zeros((far, 2 * hd), kv.dtype)
    kv[:, 2 * hd :] = jnp.ones((far + rows, hd), kv.dtype)

    greet(mate)

    def half_copy(side, base, j):
        return pltpu.make_async_remote_copy(
            src_ref=kv.at[pl.ds(base + side * half, half), pl.ds(0, 2 * hd)],
            dst_ref=kv.at[pl.ds(side * half, half), pl.ds(0, 2 * hd)],
            send_sem=half_send.at[j],
            recv_sem=half_recv.at[side],
            device_id={"ctx": j},
            device_id_type=MESH,
        )

    def second_half():
        return pltpu.make_async_remote_copy(
            src_ref=kv.at[pl.ds(far + half, half), pl.ds(0, 2 * hd)],
            dst_ref=kv.at[pl.ds(half, half), pl.ds(0, 2 * hd)],
            send_sem=half_send.at[0],
            recv_sem=half_recv.at[1],
            device_id={"ctx": 1},
            device_id_type=MESH,
        )

    def kept_copy(owner, j):
        return pltpu.make_async_remote_copy(
            src_ref=kept,
            dst_ref=kv.at[pl.ds(rows + keep * (owner - 1), keep), pl.ds(0, 2 * hd)],
            send_sem=kept_send.at[j],
            recv_sem=kept_recv.at[owner],
            device_id={"ctx": j},
            device_id_type=MESH,
        )

    def forward_copy(owner):
        slot = kv.at[pl.ds(rows + keep * (owner - 1), keep), pl.ds(0, 2 * hd)]
        return pltpu.make_async_remote_copy(
            src_ref=slot,
            dst_ref=slot,
            send_sem=forward_send.at[owner],
            recv_sem=kept_recv.at[owner],
            device_id={"ctx": mate},
            device_id_type=MESH,
        )

    loads[0].wait()
    loads[1].wait()
    loads[2].wait()
    hit = lax.broadcasted_iota(jnp.int32, (rows, keep), 0) == picks[0]
    kept[...] = lax.dot_general(
        hit.astype(jnp.float32).astype(jnp.bfloat16),
        kv[far:, 0 : 2 * hd],
        (((0,), (0,)), ((), ())),
        preferred_element_type=jnp.float32,
    ).astype(kept.dtype)

    pl.semaphore_wait(barrier, c + tps)

    def tell(i):
        pl.semaphore_signal(ready.at[h], inc=1, device_id={"ctx": 2 * i + p}, device_id_type=MESH)

    loop(0, c, tell)

    loads[3].wait()
    tall = group * turn
    contract = (((1,), (1,)), ((), ()))
    row_of = jnp.concatenate([lax.broadcasted_iota(jnp.int32, (turn, rows), 0)] * group, axis=0)
    column = lax.broadcasted_iota(jnp.int32, (tall, rows), 1)

    order = [(d % tps, sub) for d in range(1, tps + 1) for sub in range(subs)]

    def begin(step):
        d, sub = order[step]
        return pl.multiple_of(lax.rem(t + d, tps) * part + sub * turn, turn)

    def head_rows(step):
        return jnp.concatenate(
            [q[pl.ds(begin(step), turn), i * hd : (i + 1) * hd] for i in range(group)], axis=0
        )

    for step in range(len(order)):
        local_scores[step * tall : (step + 1) * tall, :] = jnp.where(
            column <= row_of + begin(step),
            lax.dot_general(
                head_rows(step), kv[far:, 0:hd], contract, preferred_element_type=jnp.float32
            ),
            -jnp.inf,
        )

    @pl.when(h == 0)
    def _():
        second_half().start()

        def serve(i):
            pl.semaphore_wait(ready.at[2 * i], 1)
            half_copy(0, far, 2 * i).start()

        loop(1, 2, serve)
        half_copy(0, far, 1).start()
        loop(2, chips, serve)

    @pl.when(h == 1)
    def _():
        half_copy(1, 0, 0).wait_recv()

        def serve(i):
            pl.semaphore_wait(ready.at[2 * i + 1], 1)
            half_copy(1, 0, 2 * i + 1).start()
            kept_copy(1, 2 * i + 1).start()

        loop(1, chips, serve)
        half_copy(0, 0, 0).wait_recv()

    @pl.when(c > 0)
    def _():
        @pl.when(p == 0)
        def _():
            kept_copy(h, h + 1).start()

        def serve(i):
            pl.semaphore_wait(ready.at[2 * i + p], 1)
            kept_copy(h, 2 * i + p).start()

        loop(c + 1, chips, serve)
        half_copy(p, 0, 0).wait_recv()
        half_copy(p, 0, mate).start()

        def forward(i):
            owner = 2 * i + p
            forward_copy(owner).wait_recv()
            forward_copy(owner).start()

        loop(1 - p, c, forward)

    @pl.when(c > 0)
    def _():
        half_copy(1 - p, 0, 0).wait_recv()
        loop(p, c + p, lambda i: forward_copy(2 * i + 1 - p).wait_recv())

    limit = jnp.where(h > 0, rows + keep * (h - 1), 0)
    bias = jnp.where(lax.broadcasted_iota(jnp.int32, (1, far), 1) < limit, 0.0, -jnp.inf)

    def out_copy(step, target, source):
        sub = order[step][1]
        return pltpu.make_async_remote_copy(
            src_ref=stage.at[pl.ds(begin(step), turn), :],
            dst_ref=out.at[pl.ds(sub * turn, turn), pl.ds(pl.multiple_of(source * width, width), width)],
            send_sem=out_send.at[step],
            recv_sem=out_recv.at[source, sub],
            device_id={"tp": target},
            device_id_type=MESH,
        )

    def own_copy(step):
        sub = order[step][1]
        return pltpu.make_async_copy(
            stage.at[pl.ds(begin(step), turn), :],
            out.at[pl.ds(sub * turn, turn), pl.ds(pl.multiple_of(t * width, width), width)],
            own_sem.at[sub],
        )

    for step in range(len(order)):
        scores = (
            lax.dot_general(
                head_rows(step), kv[0:far, 0:hd], contract, preferred_element_type=jnp.float32
            )
            + bias
        )
        own = local_scores[step * tall : (step + 1) * tall, :]
        top = jnp.maximum(
            jnp.max(scores, axis=1, keepdims=True), jnp.max(own, axis=1, keepdims=True)
        )
        weights = jnp.concatenate(
            [
                jnp.exp2((scores - top) * scale).astype(jnp.bfloat16),
                jnp.exp2((own - top) * scale).astype(jnp.bfloat16),
            ],
            axis=1,
        )
        summed = jnp.dot(weights, kv[:, hd:], preferred_element_type=jnp.float32)
        result = (summed[:, 0:hd] / summed[:, hd:]).astype(stage.dtype)
        for i in range(group):
            stage[pl.ds(begin(step), turn), i * hd : (i + 1) * hd] = result[
                i * turn : (i + 1) * turn
            ]
        d = order[step][0]
        if d:
            out_copy(step, lax.rem(t + d, tps), t).start()
        else:
            own_copy(step).start()

    @pl.when(h == 0)
    def _():
        second_half().wait_send()
        half_copy(0, far, 1).wait_send()
        loop(1, chips, lambda i: half_copy(0, far, 2 * i).wait_send())

    @pl.when(h == 1)
    def _():
        loop(1, chips, lambda i: half_copy(1, 0, 2 * i + 1).wait_send())

    @pl.when(h > 0)
    def _():
        loop(c + 1, chips, lambda i: kept_copy(h, 2 * i + p).wait_send())

    @pl.when(c > 0)
    def _():
        @pl.when(p == 0)
        def _():
            kept_copy(h, h + 1).wait_send()

        half_copy(p, 0, mate).wait_send()
        loop(1 - p, c, lambda i: forward_copy(2 * i + p).wait_send())

    for step in range(len(order)):
        d = order[step][0]
        if d:
            other = lax.rem(t + d, tps)
            out_copy(step, other, t).wait_send()
            out_copy(step, other, other).wait_recv()
        else:
            own_copy(step).wait()


def shards(n, tps, queries, key_rows, value_rows, retained):
    rows, width = queries.shape
    hd = key_rows.shape[1]
    keep = retained.shape[2]
    part = rows // tps
    turn = min(turn_rows, part)
    subs = part // turn
    far = rows + -(-(n - 2) * keep // hd) * hd
    any_spec = pl.BlockSpec(memory_space=pl.ANY)
    return pl.pallas_call(
        functools.partial(kernel, n, tps, far, turn),
        out_shape=jax.ShapeDtypeStruct((rows // tps, width * tps), queries.dtype),
        in_specs=[any_spec] * 4,
        out_specs=any_spec,
        scratch_shapes=[
            pltpu.VMEM((rows, width), jnp.bfloat16),
            pltpu.VMEM((far + rows, 3 * hd), jnp.bfloat16),
            pltpu.VMEM((keep, 2 * hd), jnp.bfloat16),
            pltpu.VMEM((1, 1, keep), jnp.int32),
            pltpu.VMEM((width // hd * rows, rows), jnp.float32),
            pltpu.VMEM((rows, width), jnp.bfloat16),
            pltpu.SemaphoreType.DMA((4,)),
            pltpu.SemaphoreType.REGULAR((n,)),
            pltpu.SemaphoreType.DMA((n,)),
            pltpu.SemaphoreType.DMA((n,)),
            pltpu.SemaphoreType.DMA((n,)),
            pltpu.SemaphoreType.DMA((n,)),
            pltpu.SemaphoreType.DMA((2,)),
            pltpu.SemaphoreType.DMA((tps * subs,)),
            pltpu.SemaphoreType.DMA((tps, subs)),
            pltpu.SemaphoreType.DMA((subs,)),
        ],
        compiler_params=pltpu.CompilerParams(
            collective_id=0, has_side_effects=True, vmem_limit_bytes=48 * 1024 * 1024
        ),
        cost_estimate=pl.CostEstimate(
            flops=4 * width * rows * (far + rows),
            bytes_accessed=4 * rows * width,
            transcendentals=width // hd * rows * (far + rows),
        ),
    )(*(pltpu.with_memory_space_constraint(x, pltpu.HBM) for x in (queries, key_rows, value_rows, retained)))


def solution(mesh):
    in_specs = (P("ctx", "tp"), P("ctx", "tp"), P("ctx", "tp"), P("ctx", "tp", None))
    out_specs = P(("ctx", "tp"), None)
    return jax.shard_map(
        functools.partial(shards, mesh.shape["ctx"], mesh.shape["tp"]),
        mesh=mesh, in_specs=in_specs, out_specs=out_specs, check_vma=False,
    )
```
